512 devices in a mesh: ctx: 64 (over z, y), tp: 8 (over x, core).
Axes of the slice: x: 4, y: 4, z: 16, core: 2. Of those that a mesh axis runs over, the one named last changes fastest.
Arguments:
- queries: bfloat16 [8192, 4096], P('ctx', 'tp'), may hold values from -10 to 10
- stretch_key_value: bfloat16 [2, 8192, 1024], P(None, 'ctx', 'tp'), may hold values from -6 to 6
- cache_kv: bfloat16 [2, 128, 2048, 1024], P(None, None, 'ctx', 'tp'), may hold values from -6 to 6
- chosen: int32 [4, 8, 3], replicated, may hold values from 0 to 127, as said below
- out_weight: bfloat16 [4096, 4096], P('ctx', 'tp'), may hold values from -0.09375 to 0.09375
Outputs:
- attention: bfloat16 [8192, 4096], P('ctx', 'tp')
- mixed: bfloat16 [8192, 4096], P('ctx', 'tp')
The draws below stay inside these ranges and needn't reach their ends.
Inputs may be any that keep to these rules, and one draw needn't show every extreme that they name: `chosen`: each row names 3 different cache blocks; some row names the first block and the last.
All inputs are finite; a program needn't handle non-finite values.
Results may differ from the reference program's by a relative error of at most 0.0052.
Values may be sent and summed in bfloat16 or wider, within the bound.
A program may use at most 64 MiB of HBM per device.

```python
import math
import jax
import jax.numpy as jnp
from jax import lax

D = 4096
QUERY_HEAD_COUNT = 32
KEY_VALUE_HEADS = 8
HEAD_SIZE = 128
BLOCK_TOKENS = 2048
CHOSEN_COUNT = 3
STRETCH_TOKENS = 8192
OWN_TOKENS = 2048
QUERY_BLOCK_COUNT = 4
CACHE_BLOCKS = 128


def draw_queries(key, part):
    key = jax.random.fold_in(key, 2)
    values_drawn = jnp.clip(2.5 * jax.random.normal(key, (STRETCH_TOKENS, QUERY_HEAD_COUNT * HEAD_SIZE), jnp.float32), -10.0, 10.0)
    return values_drawn.astype(jnp.bfloat16)


def draw_cache_kv(key, part):
    key = jax.random.fold_in(key, 3)
    complete_shape = (2, CACHE_BLOCKS, BLOCK_TOKENS, KEY_VALUE_HEADS * HEAD_SIZE)
    values_drawn = jnp.clip(jax.random.normal(key, complete_shape, jnp.float32), -6.0, 6.0)
    return values_drawn.astype(jnp.bfloat16)


def pick_blocks(pair_key):
    return jax.random.permutation(pair_key, CACHE_BLOCKS)[:CHOSEN_COUNT]


def draw_chosen(key, part):
    key = jax.random.fold_in(key, 1)
    pair_total = QUERY_BLOCK_COUNT * KEY_VALUE_HEADS
    pair_random_keys = jax.random.split(key, pair_total)
    rankings = jax.vmap(pick_blocks)(pair_random_keys).astype(jnp.int32)
    special_pair = jax.random.randint(jax.random.fold_in(key, 7), (), 0, pair_total)
    middle_block = jax.random.randint(jax.random.fold_in(key, 8), (), 1, CACHE_BLOCKS - 1)
    edge_row = jnp.stack([jnp.full((), CACHE_BLOCKS - 1, jnp.int32), jnp.zeros((), jnp.int32), middle_block.astype(jnp.int32)])
    edge_row = jnp.concatenate([edge_row, rankings[0, 3:]])[:CHOSEN_COUNT]
    is_special = (jnp.arange(pair_total) == special_pair)[:, None]
    rankings = jnp.where(is_special, edge_row[None, :], rankings)
    return rankings.reshape(QUERY_BLOCK_COUNT, KEY_VALUE_HEADS, CHOSEN_COUNT).astype(jnp.int32)


def level_of(own_key, extent, cuts, low, high):
    loudness, own = 1.0, jax.random.fold_in(own_key, 6)
    for axis_at, parts in cuts:
        draws = jnp.exp(jax.random.uniform(jax.random.fold_in(own, axis_at), (parts,), jnp.float32, low / len(cuts), high / len(cuts)))
        loudness = loudness * jnp.repeat(draws, extent[axis_at] // parts).reshape([-1 if axis == axis_at else 1 for axis in range(len(extent))])
    return loudness


def noise(rng, extent, scale, limit, shards=(), kind=jnp.bfloat16):
    entries = scale * jax.random.normal(rng, extent, jnp.float32)
    if shards:
        entries = entries * level_of(rng, extent, shards, -0.22, 0.18)
    return jnp.clip(entries, -limit, limit).astype(kind)


def setup_inputs(seed: int = 0) -> dict:
    key_of = jax.random.split(jax.random.key(seed), 6)
    return {
        "queries": draw_queries(jax.random.fold_in(key_of[5], 71), 0),
        "stretch_key_value": noise(key_of[1], (2, STRETCH_TOKENS, KEY_VALUE_HEADS * HEAD_SIZE), 1.0, 6.0, ((1, 64), (2, 8))),
        "cache_kv": draw_cache_kv(jax.random.fold_in(key_of[5], 71), 0),
        "chosen": draw_chosen(jax.random.fold_in(key_of[5], 71), 0),
        "out_weight": noise(key_of[4], (QUERY_HEAD_COUNT * HEAD_SIZE, D), (QUERY_HEAD_COUNT * HEAD_SIZE) ** -0.5, 0.09375, ((0, 64), (1, 8))),
    }


def reference(queries, stretch_key_value, cache_kv, chosen, out_weight):
    group_width = QUERY_HEAD_COUNT // KEY_VALUE_HEADS
    score_scale = 1.0 / math.sqrt(HEAD_SIZE)
    highest = lax.Precision.HIGHEST

    def single_pair(pair_position):
        block_position = (pair_position // KEY_VALUE_HEADS).astype(jnp.int32)
        group_position = (pair_position % KEY_VALUE_HEADS).astype(jnp.int32)
        zero_index = jnp.zeros((), jnp.int32)
        row_start = (block_position * OWN_TOKENS).astype(jnp.int32)
        query_rows = lax.dynamic_slice(queries, (row_start, (group_position * (group_width * HEAD_SIZE)).astype(jnp.int32)), (OWN_TOKENS, group_width * HEAD_SIZE))
        query_rows = query_rows.reshape(OWN_TOKENS, group_width, HEAD_SIZE).astype(jnp.float32)
        picked_blocks = jnp.take(cache_kv, chosen[block_position, group_position], axis=1)
        picked_blocks = lax.dynamic_slice_in_dim(picked_blocks, (group_position * HEAD_SIZE).astype(jnp.int32), HEAD_SIZE, 3)
        picked_blocks = picked_blocks.reshape(2, CHOSEN_COUNT * BLOCK_TOKENS, HEAD_SIZE).astype(jnp.float32)
        own_block = lax.dynamic_slice(stretch_key_value, (zero_index, row_start, (group_position * HEAD_SIZE).astype(jnp.int32)), (2, OWN_TOKENS, HEAD_SIZE)).astype(jnp.float32)
        far_scores = jnp.einsum('tph,kh->ptk', query_rows, picked_blocks[0], precision=highest) * score_scale
        near_scores = jnp.einsum('tph,kh->ptk', query_rows, own_block[0], precision=highest) * score_scale
        causal_mask = jnp.arange(OWN_TOKENS)[None, :] <= jnp.arange(OWN_TOKENS)[:, None]
        near_scores = jnp.where(causal_mask[None], near_scores, -jnp.inf)
        row_max = jnp.maximum(lax.optimization_barrier(jnp.max(far_scores, axis=-1)), lax.optimization_barrier(jnp.max(near_scores, axis=-1)))
        far_weights = jnp.exp(far_scores - row_max[..., None])
        near_weights = jnp.exp(near_scores - row_max[..., None])
        total_mass = lax.optimization_barrier(jnp.sum(far_weights, axis=-1)) + lax.optimization_barrier(jnp.sum(near_weights, axis=-1))
        far_rounded = lax.optimization_barrier(far_weights.astype(jnp.bfloat16)).astype(jnp.float32)
        near_rounded = lax.optimization_barrier(near_weights.astype(jnp.bfloat16)).astype(jnp.float32)
        weighted = jnp.einsum('ptk,kh->tph', far_rounded, picked_blocks[1], precision=highest)
        weighted = weighted + jnp.einsum('ptk,kh->tph', near_rounded, own_block[1], precision=highest)
        result = weighted / jnp.transpose(total_mass, (1, 0))[..., None]
        return result.astype(jnp.bfloat16).reshape(OWN_TOKENS, group_width * HEAD_SIZE)
    fragments = lax.map(single_pair, jnp.arange(QUERY_BLOCK_COUNT * KEY_VALUE_HEADS, dtype=jnp.int32))
    attention = fragments.reshape(QUERY_BLOCK_COUNT, KEY_VALUE_HEADS, OWN_TOKENS, group_width * HEAD_SIZE).transpose(0, 2, 1, 3).reshape(STRETCH_TOKENS, QUERY_HEAD_COUNT * HEAD_SIZE)
    mixed = jnp.dot(attention, out_weight, preferred_element_type=jnp.float32).astype(jnp.bfloat16)
    return (attention, mixed)
```

```python
import math

import jax
import jax.numpy as jnp
from jax import lax
from jax.experimental import pallas as pl
from jax.experimental.pallas import tpu as pltpu
from jax.sharding import PartitionSpec as P

MESH = pl.DeviceIdType.MESH
HEAD = 128
HEADS = 4
SCALE_LOG2 = math.log2(math.e) / math.sqrt(HEAD)
PIECE = 96
NEAR, OWN, CHAIN = 0, 512, 896
BF16, F32 = jnp.bfloat16, jnp.float32


def kernel(
    q_ref, skv_ref, cache_ref, chosen_ref, w_ref, att_ref, mix_ref,
    kvsend, kv, qbuf, acc, mst, lst, obuf, ost, orecv, ostr, abuf, wbuf, res, resrecv,
    s_far, s_own, s_near, s_chain, s_q, s_o, s_st, s_a, s_w0, s_wp, s_wm, s_ws, s_out,
    r_own, r_near, r_chain, r_q, r_o, r_st, r_a, r_w0, r_wp, r_wm, r_ws, r_out,
):
    ctx, tp = lax.axis_index("ctx"), lax.axis_index("tp")
    z, y, x, c = ctx // 4, ctx % 4, tp // 2, tp % 2
    qz, zq = z // 4, z % 4
    py = y % 2
    ypair = y + 1 - 2 * py
    same = c == py

    def dev(zz, yy, xx, cc):
        return (zz * 4 + yy, xx * 2 + cc)

    def rcopy(src, dst, ssem, rsem, to):
        return pltpu.make_async_remote_copy(
            src_ref=src, dst_ref=dst, send_sem=ssem, recv_sem=rsem, device_id=to, device_id_type=MESH
        )

    me = dev(z, y, x, c)

    barrier = pltpu.get_barrier_semaphore()

    def greet(to):
        pl.semaphore_signal(barrier, inc=1, device_id=to, device_id_type=MESH)

    for d in range(1, 4):
        greet(dev(4 * qz + (zq + d) % 4, y, x, c))
        greet(dev(z, (y + d) % 4, x, c))
    greet(dev((z + 1) % 16, y, x, c))
    greet(dev((z + 15) % 16, y, x, c))
    greet(dev(z, y, x, 1 - c))

    @pl.when(zq == 0)
    def _():
        for k in range(4):
            greet(dev(4 * ((qz + 3) % 4) + k, y, x, c))
        for k in (2, 3):
            greet(dev(4 * ((qz + 2) % 4) + k, y, x, c))

    @pl.when(zq == 3)
    def _():
        for k in range(4):
            greet(dev(4 * ((qz + 1) % 4) + k, y, x, c))
        for k in (0, 1):
            greet(dev(4 * ((qz + 2) % 4) + k, y, x, c))

    mine = y - py + c
    for d in range(4):
        yy = (y + d) % 4
        if d == 0:
            @pl.when(jnp.logical_not(same))
            def _():
                greet(dev(z, yy, x, py))
        else:
            greet(dev(z, yy, x, py))
        xx = (x + d) % 4
        for k in range(2):
            if d == 0:
                @pl.when(jnp.logical_not(jnp.logical_and(same, k == c)))
                def _():
                    greet(dev(z, mine, xx, k))
            else:
                greet(dev(z, mine, xx, k))
    pl.semaphore_wait(barrier, 24 - 2 * same.astype(jnp.int32))

    for b in range(4):
        for j in range(3):
            idx = chosen_ref[b, tp, j]
            kvsend[b, 0, 32 * j : 32 * j + 32] = cache_ref[0, idx]
            kvsend[b, 1, 32 * j : 32 * j + 32] = cache_ref[1, idx]

    def kvrows(first, count=PIECE):
        return kv.at[:, pl.ds(pl.multiple_of(first, 32), count), :]

    up = zq // 2
    far = [
        ((qz + 1) % 4, 0, 3 - zq),
        ((qz + 3) % 4, 3, 6 + zq),
        ((qz + 2) % 4, 3 * (1 - up), up * (7 - zq) + (1 - up) * (10 + zq)),
    ]
    far = [
        rcopy(kvsend.at[b], kvrows(CHAIN + PIECE * i), s_far.at[n], r_chain.at[i], dev(4 * b + e, y, x, c))
        for n, (b, e, i) in enumerate(far)
    ]
    for n in (2, 0, 1):
        far[n].start()
    qs = [
        rcopy(q_ref, qbuf.at[y], s_q.at[d - 1], r_q.at[d - 1], dev(z, (y + d) % 4, x, c)) for d in (1, 2, 3)
    ]
    for cp in qs:
        cp.start()
    own = [
        rcopy(
            kvsend.at[qz], kvrows(OWN + PIECE * zq), s_own.at[d - 1], r_own.at[d - 1],
            dev(4 * qz + (zq + d) % 4, y, x, c),
        )
        for d in (1, 2, 3)
    ]
    for cp in own:
        cp.start()
    near = [
        rcopy(
            skv_ref, kvrows(NEAR + 128 * zq, 128), s_near.at[d - 1], r_near.at[d - 1],
            dev(4 * qz + (zq + d) % 4, y, x, c),
        )
        for d in (1, 2, 3)
    ]
    for d in (1, 2, 3):
        pl.when(zq + d < 4)(near[d - 1].start)
    w0 = []
    for t in range(2):
        for k in range(2):
            yy = c + 2 * t
            cp = rcopy(w_ref, wbuf.at[ctx], s_w0.at[2 * t + k], r_w0.at[y], dev(z, yy, x, k))
            notself = jnp.logical_not(jnp.logical_and(yy == y, k == c))
            pl.when(notself)(cp.start)
            w0.append((cp, notself))

    qbuf[y] = q_ref[...]
    kv[:, pl.ds(pl.multiple_of(OWN + PIECE * zq, 32), PIECE), :] = kvsend[qz]
    for k in range(4):
        @pl.when(k == zq)
        def _():
            kv[:, 128 * k : 128 * k + 128, :] = skv_ref[...]

        @pl.when(k > zq)
        def _():
            kv[:, 128 * k : 128 * k + 128, :] = jnp.zeros((2, 128, HEAD), BF16)

    @pl.when(same)
    def _():
        wbuf[ctx] = w_ref[...]

    mst[...] = jnp.full(mst.shape, -1e30, F32)
    lst[...] = jnp.zeros(lst.shape, F32)
    acc[...] = jnp.zeros(acc.shape, F32)

    def chain(i):
        for idx, ok, to in ((i, zq < 3, z + 1), (6 + i, zq > 0, z - 1)):
            rows = kvrows(CHAIN + PIECE * idx)
            cp = rcopy(rows, rows, s_chain.at[idx], r_chain.at[idx], dev(to, y, x, c))
            cp.wait_recv()
            pl.when(ok)(cp.start)

    def chain_sent(i):
        for idx, ok, to in ((i, zq < 3, z + 1), (6 + i, zq > 0, z - 1)):
            rows = kvrows(CHAIN + PIECE * idx)
            cp = rcopy(rows, rows, s_chain.at[idx], r_chain.at[idx], dev(to, y, x, c))
            pl.when(ok)(cp.wait_send)

    def wblock(origin):
        return wbuf.at[pl.ds(4 * ((origin + 32) % 16) + 2 * c, 2)]

    def wcopies(t):
        up_block, down_block = wblock(z - (t - 1)), wblock(z + (t - 1))
        ups = rcopy(up_block, up_block, s_wp.at[t - 1], r_wp.at[t - 1], dev((z + 1) % 16, y, x, c))
        downs = None
        if t <= 7:
            downs = rcopy(down_block, down_block, s_wm.at[t - 1], r_wm.at[t - 1], dev((z + 15) % 16, y, x, c))
        return ups, downs

    def wsibling(t):
        sib = dev(z, y, x, 1 - c)
        ub, db = wblock(z - t), wblock(z + t)
        out = [rcopy(ub, ub, s_ws.at[t - 1], r_ws.at[t - 1], sib)]
        if t <= 7:
            out.append(rcopy(db, db, s_ws.at[7 + t], r_ws.at[7 + t], sib))
        return out

    def wstart(t):
        for cp in wcopies(t):
            if cp is not None:
                cp.start()

    def wstep(t):
        for cp in wcopies(t):
            if cp is not None:
                cp.wait_recv()
        if t < 8:
            wstart(t + 1)
        for cp in wsibling(t):
            cp.start()

    def attend(first, count, masked):
        def one(h, _):
            qh = qbuf[:, :, pl.ds(pl.multiple_of(h * HEAD, HEAD), HEAD)].reshape(512, HEAD)
            s = lax.dot_general(
                kv[0, first : first + count], qh, (((1,), (1,)), ((), ())), preferred_element_type=F32
            )
            if masked:
                key = lax.broadcasted_iota(jnp.int32, (count, 512), 0)
                row = lax.broadcasted_iota(jnp.int32, (count, 512), 1)
                pos = (key // 128) * 512 + y * 128 + key % 128
                s = jnp.where(pos <= row + 512 * zq, s, -jnp.inf)
            before = mst[h]
            top = jnp.maximum(before, jnp.max(s, axis=0, keepdims=True))
            p = jnp.exp2((s - top) * SCALE_LOG2)
            shrink = jnp.exp2((before - top) * SCALE_LOG2)
            mst[h] = top
            lst[h] = lst[h] * shrink + jnp.sum(p, axis=0, keepdims=True)
            acc[h] = acc[h] * shrink + lax.dot_general(
                kv[1, first : first + count], p.astype(BF16), (((0,), (0,)), ((), ())),
                preferred_element_type=F32,
            )
            return 0

        lax.fori_loop(0, HEADS, one, 0)

    for cp in qs:
        cp.wait_recv()
    for i in range(6):
        chain(i)
    for cp, ns in w0:
        pass
    for k in range(4):
        cp = rcopy(w_ref, wbuf.at[4 * z + k], s_w0.at[0], r_w0.at[k], me)
        pl.when(jnp.logical_not(jnp.logical_and(same, k == y)))(cp.wait_recv)
    wstart(1)
    for cp in own:
        cp.wait_recv()
    attend(OWN, 384, False)
    wstep(1)
    for d in (1, 2, 3):
        pl.when(zq >= d)(near[d - 1].wait_recv)
    attend(NEAR, 512, True)
    wstep(2)
    attend(CHAIN, 576, False)
    wstep(3)
    attend(CHAIN + 576, 576, False)

    def finish(h, _):
        o = acc[h] * (1.0 / lst[h])
        for r in range(4):
            obuf[r, h] = o[:, r * 128 : r * 128 + 128].astype(BF16)
            ost[r, h] = mst[h][:, r * 128 : r * 128 + 128]
            ost[r, HEADS + h] = lst[h][:, r * 128 : r * 128 + 128]
        return 0

    lax.fori_loop(0, HEADS, finish, 0)
    ocp, scp = [], []
    for d in (1, 2, 3):
        r = (y + d) % 4
        ocp.append(rcopy(obuf.at[r], orecv.at[d - 1], s_o.at[d - 1], r_o.at[d - 1], dev(z, r, x, c)))
        scp.append(rcopy(ost.at[r], ostr.at[d - 1], s_st.at[d - 1], r_st.at[d - 1], dev(z, r, x, c)))
    for n in (1, 0, 2):
        scp[n].start()
        ocp[n].start()
    wstep(4)
    for n in range(3):
        scp[n].wait_recv()
        ocp[n].wait_recv()

    for h in range(HEADS):
        ms = [ost[y, h]] + [ostr[n, h] for n in range(3)]
        ls = [ost[y, HEADS + h]] + [ostr[n, HEADS + h] for n in range(3)]
        os_ = [obuf[y, h]] + [orecv[n, h] for n in range(3)]
        top = jnp.maximum(jnp.maximum(ms[0], ms[1]), jnp.maximum(ms[2], ms[3]))
        ws = [l * jnp.exp2((m - top) * SCALE_LOG2) for m, l in zip(ms, ls)]
        inv = 1.0 / (ws[0] + ws[1] + ws[2] + ws[3])
        o = sum(o_.astype(F32) * (w * inv) for o_, w in zip(os_, ws))
        att_ref[:, h * HEAD : h * HEAD + HEAD] = o.T.astype(BF16)

    acp = []
    for d in (2, 1, 3, 0):
        xx = (x + d) % 4
        for t in range(2):
            yy = ypair if t == 0 else y
            cp = rcopy(att_ref, abuf.at[tp], s_a.at[2 * d + t], r_a.at[tp], dev(z, yy, xx, py))
            if d == 0 and t == 1:
                pl.when(jnp.logical_not(same))(cp.start)
            else:
                cp.start()
            acp.append((cp, d == 0 and t == 1))

    @pl.when(same)
    def _():
        abuf[tp] = att_ref[...]

    for t in (5, 6, 7, 8):
        wstep(t)
    for g in range(8):
        cp = rcopy(att_ref, abuf.at[g], s_a.at[0], r_a.at[g], me)
        pl.when(jnp.logical_not(jnp.logical_and(same, tp == g)))(cp.wait_recv)
    for t in range(1, 9):
        for n, cp in enumerate(wsibling(t)):
            ob = 4 * ((z - t + 32) % 16 if n == 0 else (z + t) % 16) + 2 * (1 - c)
            blk = wbuf.at[pl.ds(ob, 2)]
            rcopy(blk, blk, s_ws.at[0], r_ws.at[t - 1 if n == 0 else 7 + t], me).wait_recv()

    def project(g, total):
        return total + jnp.dot(abuf[g], wbuf[pl.ds(8 * g, 8)].reshape(512, 512), preferred_element_type=F32)

    res[...] = lax.fori_loop(0, 8, project, jnp.zeros((128, 512), F32)).astype(BF16)
    out = rcopy(res, resrecv, s_out.at[0], r_out.at[0], dev(z, ypair, x, 1 - c))

    @pl.when(same)
    def _():
        mix_ref[...] = res[...]

    @pl.when(jnp.logical_not(same))
    def _():
        out.start()
        out.wait()
        mix_ref[...] = resrecv[...]

    for cp in far + qs + own + ocp + scp:
        cp.wait_send()
    for d in (1, 2, 3):
        pl.when(zq + d < 4)(near[d - 1].wait_send)
    for cp, ns in w0:
        pl.when(ns)(cp.wait_send)
    for i in range(6):
        chain_sent(i)
    for cp, maybe in acp:
        if maybe:
            pl.when(jnp.logical_not(same))(cp.wait_send)
        else:
            cp.wait_send()
    for t in range(1, 9):
        for cp in wcopies(t):
            if cp is not None:
                cp.wait_send()
        for cp in wsibling(t):
            cp.wait_send()


def body(queries, stretch_key_value, cache_kv, chosen, out_weight):
    dma = lambda n: pltpu.SemaphoreType.DMA((n,))
    vmem = pl.BlockSpec(memory_space=pltpu.VMEM)
    return pl.pallas_call(
        kernel,
        out_shape=(jax.ShapeDtypeStruct((128, 512), BF16), jax.ShapeDtypeStruct((128, 512), BF16)),
        in_specs=[vmem, vmem, vmem, pl.BlockSpec(memory_space=pltpu.SMEM), vmem],
        out_specs=(vmem, vmem),
        scratch_shapes=[
            pltpu.VMEM((4, 2, PIECE, HEAD), BF16),
            pltpu.VMEM((2, 2048, HEAD), BF16),
            pltpu.VMEM((4, 128, 512), BF16),
            pltpu.VMEM((HEADS, HEAD, 512), F32),
            pltpu.VMEM((HEADS, 1, 512), F32),
            pltpu.VMEM((HEADS, 1, 512), F32),
            pltpu.VMEM((4, HEADS, HEAD, 128), BF16),
            pltpu.VMEM((4, 2 * HEADS, 1, 128), F32),
            pltpu.VMEM((3, HEADS, HEAD, 128), BF16),
            pltpu.VMEM((3, 2 * HEADS, 1, 128), F32),
            pltpu.VMEM((8, 128, 512), BF16),
            pltpu.VMEM((64, 64, 512), BF16),
            pltpu.VMEM((128, 512), BF16),
            pltpu.VMEM((128, 512), BF16),
        ]
        + [dma(n) for n in (3, 3, 3, 12, 3, 3, 3, 8, 4, 8, 7, 15, 1)]
        + [dma(n) for n in (3, 3, 12, 3, 3, 3, 8, 4, 8, 7, 15, 1)],
        compiler_params=pltpu.CompilerParams(
            collective_id=0, has_side_effects=True, vmem_limit_bytes=56 * 2**20
        ),
        cost_estimate=pl.CostEstimate(flops=2 * 2**30, bytes_accessed=4 * 2**20, transcendentals=2**22),
    )(queries, stretch_key_value, cache_kv, chosen, out_weight)


def solution(mesh):
    in_specs = (
        P("ctx", "tp"),
        P(None, "ctx", "tp"),
        P(None, None, "ctx", "tp"),
        P(),
        P("ctx", "tp"),
    )
    out_specs = (P("ctx", "tp"), P("ctx", "tp"))
    return jax.shard_map(body, mesh=mesh, in_specs=in_specs, out_specs=out_specs, check_vma=False)
```

```python
import math

import jax
import jax.numpy as jnp
from jax import lax
from jax.experimental import pallas as pl
from jax.experimental.pallas import tpu as pltpu
from jax.sharding import PartitionSpec as P

MESH = pl.DeviceIdType.MESH
HEAD = 128
HEADS = 4
SCALE_LOG2 = math.log2(math.e) / math.sqrt(HEAD)
PIECE = 96
NEAR, OWN, CHAIN = 0, 512, 896
PARTS = 2
SLOTS = ((0,"w"),(0,""),(0,""),(0,""),(0,"q o O"),(0,"r n"),(0,"N"),(1,""),(0,"A"),(1,""),(0,"C"),(1,""),(0,"B"),(1,""),(0,""),(1,"D"))
LAG = 3
MID, LATE = (1,3), (3,3)
BF16, F32 = jnp.bfloat16, jnp.float32


def kernel(
    q_ref, skv_ref, cache_ref, chosen_ref, w_ref, att_ref, mix_ref,
    kvsend, kv, qsend, qbuf, acc, mst, lst, obuf, ost, orecv, ostr, abuf, abuf_out, wbuf, res, resrecv,
    s_far, s_own, s_near, s_chain, s_q, s_o, s_st, s_a, s_w0, s_w, s_out,
    r_own, r_near, r_chain, r_q, r_o, r_st, r_a, r_w0, r_wp, r_wm, r_ws, r_out,
):
    ctx, tp = lax.axis_index("ctx"), lax.axis_index("tp")
    z, y, x, c = ctx // 4, ctx % 4, tp // 2, tp % 2
    qz, zq = z // 4, z % 4
    py = y % 2
    ypair = y + 1 - 2 * py
    same = c == py

    def dev(zz, yy, xx, cc):
        return (zz * 4 + yy, xx * 2 + cc)

    def rcopy(src, dst, ssem, rsem, to):
        return pltpu.make_async_remote_copy(
            src_ref=src, dst_ref=dst, send_sem=ssem, recv_sem=rsem, device_id=to, device_id_type=MESH
        )

    me = dev(z, y, x, c)

    barrier = pltpu.get_barrier_semaphore()

    def greet(to):
        pl.semaphore_signal(barrier, inc=1, device_id=to, device_id_type=MESH)

    for d in range(1, 4):
        greet(dev(4 * qz + (zq + d) % 4, y, x, c))
        greet(dev(z, (y + d) % 4, x, c))
    greet(dev((z + 1) % 16, y, x, c))
    greet(dev((z + 15) % 16, y, x, c))
    greet(dev(z, y, x, 1 - c))

    @pl.when(zq == 0)
    def _():
        for k in range(4):
            greet(dev(4 * ((qz + 3) % 4) + k, y, x, c))
        for k in (2, 3):
            greet(dev(4 * ((qz + 2) % 4) + k, y, x, c))

    @pl.when(zq == 3)
    def _():
        for k in range(4):
            greet(dev(4 * ((qz + 1) % 4) + k, y, x, c))
        for k in (0, 1):
            greet(dev(4 * ((qz + 2) % 4) + k, y, x, c))

    mine = y - py + c
    for d in range(4):
        yy = (y + d) % 4
        if d == 0:
            @pl.when(jnp.logical_not(same))
            def _():
                greet(dev(z, yy, x, py))
        else:
            greet(dev(z, yy, x, py))
        xx = (x + d) % 4
        for k in range(2):
            if d == 0:
                @pl.when(jnp.logical_not(jnp.logical_and(same, k == c)))
                def _():
                    greet(dev(z, mine, xx, k))
            else:
                greet(dev(z, mine, xx, k))
    pl.semaphore_wait(barrier, 24 - 2 * same.astype(jnp.int32))

    for b in range(4):
        for j in range(3):
            idx = chosen_ref[j, b, tp]
            kvsend[b, 0, 32 * j : 32 * j + 32] = cache_ref[0, idx]
            kvsend[b, 1, 32 * j : 32 * j + 32] = cache_ref[1, idx]

    def kvrows(first, count=PIECE):
        return kv.at[:, pl.ds(pl.multiple_of(first, 32), count), :]

    up = zq // 2
    far = [
        ((qz + 1) % 4, 0, 3 - zq),
        ((qz + 3) % 4, 3, 6 + zq),
        ((qz + 2) % 4, 3 * (1 - up), up * (7 - zq) + (1 - up) * (10 + zq)),
    ]
    far = [
        rcopy(kvsend.at[b], kvrows(CHAIN + PIECE * i), s_far.at[n], r_chain.at[i], dev(4 * b + e, y, x, c))
        for n, (b, e, i) in enumerate(far)
    ]
    for n in (2, 0, 1):
        far[n].start()
    for h in range(HEADS):
        qsend[h] = q_ref[:, h * HEAD : h * HEAD + HEAD]
    my_rows = qbuf.at[:, pl.ds(pl.multiple_of(128 * y, 128), 128), :]
    qs = [
        rcopy(qsend, my_rows, s_q.at[d - 1], r_q.at[d - 1], dev(z, (y + d) % 4, x, c)) for d in (1, 2, 3)
    ]
    for cp in qs:
        cp.start()
    own = [
        rcopy(
            kvsend.at[qz], kvrows(OWN + PIECE * zq), s_own.at[d - 1], r_own.at[d - 1],
            dev(4 * qz + (zq + d) % 4, y, x, c),
        )
        for d in (1, 2, 3)
    ]
    for cp in own:
        cp.start()
    near = [
        rcopy(
            skv_ref, kvrows(NEAR + 128 * zq, 128), s_near.at[d - 1], r_near.at[d - 1],
            dev(4 * qz + (zq + d) % 4, y, x, c),
        )
        for d in (1, 2, 3)
    ]
    for d in (1, 2, 3):
        pl.when(zq + d < 4)(near[d - 1].start)
    w0 = []
    for t in range(2):
        for k in range(2):
            yy = c + 2 * t
            cp = rcopy(w_ref, wbuf.at[ctx], s_w0.at[2 * t + k], r_w0.at[y], dev(z, yy, x, k))
            w0.append((cp, jnp.logical_not(jnp.logical_and(yy == y, k == c))))

    def w0_send():
        for cp, notself in w0:
            pl.when(notself)(cp.start)

    qbuf[:, pl.ds(pl.multiple_of(128 * y, 128), 128), :] = qsend[...]
    kv[:, pl.ds(pl.multiple_of(OWN + PIECE * zq, 32), PIECE), :] = kvsend[qz]
    for k in range(4):
        @pl.when(k == zq)
        def _():
            kv[:, 128 * k : 128 * k + 128, :] = skv_ref[...]

        @pl.when(k > zq)
        def _():
            kv[:, 128 * k : 128 * k + 128, :] = jnp.zeros((2, 128, HEAD), BF16)

    @pl.when(same)
    def _():
        wbuf[ctx] = w_ref[...]

    mst[...] = jnp.full(mst.shape, -1e30, F32)
    lst[...] = jnp.zeros(lst.shape, F32)
    acc[...] = jnp.zeros(acc.shape, F32)

    def link(idx, to):
        rows = kvrows(CHAIN + PIECE * idx)
        return rcopy(rows, rows, s_chain.at[idx // 6], r_chain.at[idx], dev(to, y, x, c))

    def chain(slot):
        for i, base, ok, to in (
            (slot - LAG * zq, 0, zq < 3, z + 1), (slot - LAG * (3 - zq), 6, zq > 0, z - 1)
        ):
            @pl.when(jnp.logical_and(i >= 0, i < 6))
            def _():
                cp = link(base + i, to)
                cp.wait_recv()
                pl.when(ok)(cp.start)

    def chain_sent():
        for n, ok in enumerate((zq < 3, zq > 0)):
            every = kvrows(CHAIN, 6 * PIECE)
            pl.when(ok)(rcopy(every, every, s_chain.at[n], r_chain.at[0], me).wait_send)

    sib = dev(z, y, x, 1 - c)

    def wpart(origin, j, cc):
        per = PARTS // 2
        rows = 64 // per
        first = pl.multiple_of(rows * (j % per), rows)
        return wbuf.at[4 * ((origin + 32) % 16) + 2 * cc + j // per, pl.ds(first, rows)]

    def wsend(e, way):
        t, j = e // PARTS, e % PARTS
        part = wpart(z - t if way else z + t, j, c)
        ssem, rsem = (s_w.at[0], r_wp) if way else (s_w.at[1], r_wm)
        return rcopy(part, part, ssem, rsem.at[e], dev((z + (1 if way else 15)) % 16, y, x, c))

    def wshare(t, way):
        block = wbuf.at[pl.ds(4 * (((z - t if way else z + t) + 32) % 16) + 2 * c, 2)]
        return rcopy(block, block, s_w.at[2], r_ws.at[0], sib)

    def wstart():
        def one(e, _):
            wsend(e, True).start()
            wsend(e, False).start()
            return 0

        lax.fori_loop(0, PARTS, one, 0)

    def wevents(first, last):
        def one(e, _):
            wsend(e, True).wait_recv()
            pl.when(e < 7 * PARTS)(wsend(e + PARTS, True).start)

            @pl.when(e < 7 * PARTS)
            def _():
                wsend(e, False).wait_recv()
                pl.when(e < 6 * PARTS)(wsend(e + PARTS, False).start)

            @pl.when(e % PARTS == PARTS - 1)
            def _():
                wshare(e // PARTS + 1, True).start()
                pl.when(e < 7 * PARTS)(wshare(e // PARTS + 1, False).start)

            return 0

        lax.fori_loop(first, last, one, 0)

    def wfinish():
        every = wbuf.at[pl.ds(0, 30)]
        rcopy(every, every, s_w.at[2], r_ws.at[0], sib).wait_recv()

    def wsent():
        for n, count in enumerate((16, 14, 30)):
            every = wbuf.at[pl.ds(0, count)]
            rcopy(every, every, s_w.at[n], r_ws.at[0], sib).wait_send()

    def attend(first, count, masked=False):
        rows = pl.ds(first if isinstance(first, int) else pl.multiple_of(first, 32), count)
        q = qbuf[...].reshape(HEADS * 512, HEAD)
        s = lax.dot_general(kv[0, rows], q, (((1,), (1,)), ((), ())), preferred_element_type=F32)
        if masked:
            key = lax.broadcasted_iota(jnp.int32, s.shape, 0)
            row = lax.broadcasted_iota(jnp.int32, s.shape, 1) % 512
            pos = (key // 128) * 512 + y * 128 + key % 128
            s = jnp.where(pos <= row + 512 * zq, s, -jnp.inf)
        before = mst[...]
        top = jnp.maximum(before, jnp.max(s, axis=0, keepdims=True))
        p = jnp.exp2((s - top) * SCALE_LOG2)
        shrink = jnp.exp2((before - top) * SCALE_LOG2)
        mst[...] = top
        lst[...] = lst[...] * shrink + jnp.sum(p, axis=0, keepdims=True)
        acc[...] = acc[...] * shrink + lax.dot_general(
            kv[1, rows], p.astype(BF16), (((0,), (0,)), ((), ())), preferred_element_type=F32
        )

    half = 3 * PIECE
    at = 0
    one_way = CHAIN + 6 * PIECE * (zq // 2)
    other_way = CHAIN + 6 * PIECE * (1 - zq // 2)
    def w0_wait(first):
        for k in range(2):
            yy = first + k
            cp = rcopy(w_ref, wbuf.at[4 * z + yy], s_w0.at[0], r_w0.at[yy], me)
            pl.when(jnp.logical_not(jnp.logical_and(same, yy == y)))(cp.wait_recv)

    def got_queries():
        for cp in qs:
            cp.wait_recv()

    def got_own():
        for cp in own:
            cp.wait_recv()

    def got_near():
        for d in (1, 2, 3):
            pl.when(zq >= d)(near[d - 1].wait_recv)

    def ring_begin():
        w0_wait(2 * c)
        wstart()

    work = {
        "w": w0_send, "q": got_queries, "o": got_own, "n": got_near, "r": ring_begin,
        "O": lambda: attend(OWN, 4 * PIECE),
        "N": lambda: attend(NEAR, 512, True),
        "A": lambda: attend(one_way, half),
        "B": lambda: attend(other_way, half),
        "C": lambda: attend(one_way + half, half),
        "D": lambda: attend(other_way + half, half),
    }
    for slot, (events, todo) in enumerate(SLOTS):
        if slot < 6 + 3 * LAG:
            chain(slot)
        for name in todo.split():
            work[name]()
        wevents(at, at + events)
        at += events

    ocp, scp = [], []
    for r in range(4):
        for h in range(HEADS):
            cols = slice(512 * h + 128 * r, 512 * h + 128 * r + 128)
            ost[r, h] = mst[:, cols]
            ost[r, HEADS + h] = lst[:, cols]
    for d in (2, 1, 3):
        r = (y + d) % 4
        scp.append(rcopy(ost.at[r], ostr.at[d - 1], s_st.at[d - 1], r_st.at[d - 1], dev(z, r, x, c)))
        scp[-1].start()
    for k in range(2):
        for h in (2 * k, 2 * k + 1):
            cols = slice(512 * h, 512 * h + 512)
            o = acc[:, cols] * (1.0 / lst[:, cols])
            for r in range(4):
                obuf[k, r, h % 2] = o[:, r * 128 : r * 128 + 128].astype(BF16)
        for d in (2, 1, 3):
            r, n = (y + d) % 4, 3 * k + d - 1
            ocp.append(rcopy(obuf.at[k, r], orecv.at[k, d - 1], s_o.at[n], r_o.at[n], dev(z, r, x, c)))
            ocp[-1].start()
        wevents(at, at + MID[k])
        at += MID[k]

    for k in range(2):
        for cp in (scp if k == 0 else []) + ocp[3 * k : 3 * k + 3]:
            cp.wait_recv()
        for h in range(2):
            ms = [ost[y, 2 * k + h]] + [ostr[n, 2 * k + h] for n in range(3)]
            ls = [ost[y, HEADS + 2 * k + h]] + [ostr[n, HEADS + 2 * k + h] for n in range(3)]
            os_ = [obuf[k, y, h]] + [orecv[k, n, h] for n in range(3)]
            top = jnp.maximum(jnp.maximum(ms[0], ms[1]), jnp.maximum(ms[2], ms[3]))
            ws = [l * jnp.exp2((m - top) * SCALE_LOG2) for m, l in zip(ms, ls)]
            inv = 1.0 / (ws[0] + ws[1] + ws[2] + ws[3])
            o = sum(o_.astype(F32) * (w * inv) for o_, w in zip(os_, ws))
            o = o.T.astype(BF16)
            abuf_out[k, :, h * HEAD : h * HEAD + HEAD] = o
            att_ref[:, (2 * k + h) * HEAD : (2 * k + h + 1) * HEAD] = o
        for d in (2, 1, 3, 0):
            for t in range(2):
                to = dev(z, ypair if t == 0 else y, (x + d) % 4, py)
                cp = rcopy(abuf_out.at[k], abuf.at[tp, k], s_a.at[0], r_a.at[0], to)
                if d == 0 and t == 1:
                    pl.when(jnp.logical_not(same))(cp.start)
                else:
                    cp.start()

        @pl.when(same)
        def _():
            abuf[tp, k] = abuf_out[k]

        wevents(at, at + LATE[k])
        at += LATE[k]

    wevents(at, 8 * PARTS)
    w0_wait(2 * (1 - c))
    wfinish()
    def every_a(count):
        return rcopy(abuf.at[pl.ds(0, count)], abuf.at[pl.ds(0, count)], s_a.at[0], r_a.at[0], sib)

    pl.when(same)(every_a(7).wait_recv)
    pl.when(jnp.logical_not(same))(every_a(8).wait_recv)

    def project(g, total):
        for k in range(2):
            w = wbuf[pl.ds(8 * g + 4 * k, 4)].reshape(256, 512)
            total = total + jnp.dot(abuf[g, k], w, preferred_element_type=F32)
        return total

    res[...] = lax.fori_loop(0, 8, project, jnp.zeros((128, 512), F32)).astype(BF16)
    out = rcopy(res, resrecv, s_out.at[0], r_out.at[0], dev(z, ypair, x, 1 - c))

    @pl.when(same)
    def _():
        mix_ref[...] = res[...]

    @pl.when(jnp.logical_not(same))
    def _():
        out.start()
        out.wait()
        mix_ref[...] = resrecv[...]

    for cp in far + qs + own + scp + ocp:
        cp.wait_send()
    for d in (1, 2, 3):
        pl.when(zq + d < 4)(near[d - 1].wait_send)
    for cp, ns in w0:
        pl.when(ns)(cp.wait_send)
    chain_sent()
    pl.when(same)(every_a(7).wait_send)
    pl.when(jnp.logical_not(same))(every_a(8).wait_send)
    wsent()


def body(queries, stretch_key_value, cache_kv, chosen, out_weight):
    dma = lambda n: pltpu.SemaphoreType.DMA((n,))
    vmem = pl.BlockSpec(memory_space=pltpu.VMEM)
    return pl.pallas_call(
        kernel,
        out_shape=(jax.ShapeDtypeStruct((128, 512), BF16), jax.ShapeDtypeStruct((128, 512), BF16)),
        in_specs=[vmem, vmem, vmem, pl.BlockSpec(memory_space=pltpu.SMEM), vmem],
        out_specs=(vmem, vmem),
        scratch_shapes=[
            pltpu.VMEM((4, 2, PIECE, HEAD), BF16),
            pltpu.VMEM((2, 2048, HEAD), BF16),
            pltpu.VMEM((HEADS, 128, HEAD), BF16),
            pltpu.VMEM((HEADS, 512, HEAD), BF16),
            pltpu.VMEM((HEAD, HEADS * 512), F32),
            pltpu.VMEM((1, HEADS * 512), F32),
            pltpu.VMEM((1, HEADS * 512), F32),
            pltpu.VMEM((2, 4, 2, HEAD, 128), BF16),
            pltpu.VMEM((4, 2 * HEADS, 1, 128), F32),
            pltpu.VMEM((2, 3, 2, HEAD, 128), BF16),
            pltpu.VMEM((3, 2 * HEADS, 1, 128), F32),
            pltpu.VMEM((8, 2, 128, 256), BF16),
            pltpu.VMEM((2, 128, 256), BF16),
            pltpu.VMEM((64, 64, 512), BF16),
            pltpu.VMEM((128, 512), BF16),
            pltpu.VMEM((128, 512), BF16),
        ]
        + [dma(n) for n in (3, 3, 3, 2, 3, 6, 3, 1, 4, 3, 1)]
        + [dma(n) for n in (3, 3, 12, 3, 6, 3, 1, 4, 8 * PARTS, 7 * PARTS, 1, 1)],
        compiler_params=pltpu.CompilerParams(
            collective_id=0, has_side_effects=True, vmem_limit_bytes=56 * 2**20
        ),
        cost_estimate=pl.CostEstimate(flops=2 * 2**30, bytes_accessed=4 * 2**20, transcendentals=2**22),
    )(queries, stretch_key_value, cache_kv, chosen.transpose(2, 0, 1), out_weight)


def solution(mesh):
    in_specs = (
        P("ctx", "tp"),
        P(None, "ctx", "tp"),
        P(None, None, "ctx", "tp"),
        P(),
        P("ctx", "tp"),
    )
    out_specs = (P("ctx", "tp"), P("ctx", "tp"))
    return jax.shard_map(body, mesh=mesh, in_specs=in_specs, out_specs=out_specs, check_vma=False)
```

```python
import math

import jax
import jax.numpy as jnp
from jax import lax
from jax.experimental import pallas as pl
from jax.experimental.pallas import tpu as pltpu
from jax.sharding import PartitionSpec as P

MESH = pl.DeviceIdType.MESH
HEAD = 128
HEADS = 4
SCALE_LOG2 = math.log2(math.e) / math.sqrt(HEAD)
PIECE = 96
NEAR, OWN, CHAIN = 0, 512, 896
PARTS = 2
SLOTS = ((0,"w"),(0,""),(0,""),(0,""),(0,"q o O"),(0,"r n"),(0,"N"),(1,""),(0,"A"),(1,""),(0,"C"),(1,""),(0,"B"),(1,""),(0,""),(1,"D"))
LAG = 3
MID, LATE = (1,3), (3,3)
BF16, F32 = jnp.bfloat16, jnp.float32


def kernel(
    q_ref, skv_ref, cache_ref, chosen_ref, w_ref, att_ref, mix_ref,
    kvsend, kv, qsend, qbuf, acc, mst, lst, obuf, ost, orecv, ostr, abuf, abuf_out, wbuf, res, resrecv,
    s_far, s_own, s_near, s_chain, s_q, s_o, s_st, s_a, s_w0, s_w, s_out,
    r_own, r_near, r_chain, r_q, r_o, r_st, r_a, r_w0, r_wp, r_wm, r_ws, r_out,
):
    ctx, tp = lax.axis_index("ctx"), lax.axis_index("tp")
    z, y, x, c = ctx // 4, ctx % 4, tp // 2, tp % 2
    qz, zq = z // 4, z % 4
    py = y % 2
    ypair = y + 1 - 2 * py
    same = c == py

    def dev(zz, yy, xx, cc):
        return (zz * 4 + yy, xx * 2 + cc)

    def rcopy(src, dst, ssem, rsem, to):
        return pltpu.make_async_remote_copy(
            src_ref=src, dst_ref=dst, send_sem=ssem, recv_sem=rsem, device_id=to, device_id_type=MESH
        )

    me = dev(z, y, x, c)

    barrier = pltpu.get_barrier_semaphore()

    def greet(to):
        pl.semaphore_signal(barrier, inc=1, device_id=to, device_id_type=MESH)

    for d in range(1, 4):
        greet(dev(4 * qz + (zq + d) % 4, y, x, c))
        greet(dev(z, (y + d) % 4, x, c))
    greet(dev((z + 1) % 16, y, x, c))
    greet(dev((z + 15) % 16, y, x, c))
    greet(dev(z, y, x, 1 - c))

    @pl.when(zq == 0)
    def _():
        for k in range(4):
            greet(dev(4 * ((qz + 3) % 4) + k, y, x, c))
        for k in (2, 3):
            greet(dev(4 * ((qz + 2) % 4) + k, y, x, c))

    @pl.when(zq == 3)
    def _():
        for k in range(4):
            greet(dev(4 * ((qz + 1) % 4) + k, y, x, c))
        for k in (0, 1):
            greet(dev(4 * ((qz + 2) % 4) + k, y, x, c))

    mine = y - py + c
    for d in range(4):
        yy = (y + d) % 4
        if d == 0:
            @pl.when(jnp.logical_not(same))
            def _():
                greet(dev(z, yy, x, py))
        else:
            greet(dev(z, yy, x, py))
        xx = (x + d) % 4
        for k in range(2):
            if d == 0:
                @pl.when(jnp.logical_not(jnp.logical_and(same, k == c)))
                def _():
                    greet(dev(z, mine, xx, k))
            else:
                greet(dev(z, mine, xx, k))
    pl.semaphore_wait(barrier, 24 - 2 * same.astype(jnp.int32))

    for b in range(4):
        for j in range(3):
            idx = chosen_ref[j, b, tp]
            kvsend[b, 0, 32 * j : 32 * j + 32] = cache_ref[0, idx]
            kvsend[b, 1, 32 * j : 32 * j + 32] = cache_ref[1, idx]

    def kvrows(first, count=PIECE):
        return kv.at[:, pl.ds(pl.multiple_of(first, 32), count), :]

    up = zq // 2
    far = [
        ((qz + 1) % 4, 0, 3 - zq),
        ((qz + 3) % 4, 3, 6 + zq),
        ((qz + 2) % 4, 3 * (1 - up), up * (7 - zq) + (1 - up) * (10 + zq)),
    ]
    far = [
        rcopy(kvsend.at[b], kvrows(CHAIN + PIECE * i), s_far.at[n], r_chain.at[i], dev(4 * b + e, y, x, c))
        for n, (b, e, i) in enumerate(far)
    ]
    for n in (2, 0, 1):
        far[n].start()
    for h in range(HEADS):
        qsend[h] = q_ref[:, h * HEAD : h * HEAD + HEAD]
    my_rows = qbuf.at[:, pl.ds(pl.multiple_of(128 * y, 128), 128), :]
    qs = [
        rcopy(qsend, my_rows, s_q.at[d - 1], r_q.at[d - 1], dev(z, (y + d) % 4, x, c)) for d in (1, 2, 3)
    ]
    for cp in qs:
        cp.start()
    own = [
        rcopy(
            kvsend.at[qz], kvrows(OWN + PIECE * zq), s_own.at[d - 1], r_own.at[d - 1],
            dev(4 * qz + (zq + d) % 4, y, x, c),
        )
        for d in (1, 2, 3)
    ]
    for cp in own:
        cp.start()
    near = [
        rcopy(
            skv_ref, kvrows(NEAR + 128 * zq, 128), s_near.at[d - 1], r_near.at[d - 1],
            dev(4 * qz + (zq + d) % 4, y, x, c),
        )
        for d in (1, 2, 3)
    ]
    for d in (1, 2, 3):
        pl.when(zq + d < 4)(near[d - 1].start)
    w0 = []
    for t in range(2):
        for k in range(2):
            yy = c + 2 * t
            cp = rcopy(w_ref, wbuf.at[ctx], s_w0.at[2 * t + k], r_w0.at[y], dev(z, yy, x, k))
            w0.append((cp, jnp.logical_not(jnp.logical_and(yy == y, k == c))))

    def w0_send():
        for cp, notself in w0:
            pl.when(notself)(cp.start)

    qbuf[:, pl.ds(pl.multiple_of(128 * y, 128), 128), :] = qsend[...]
    kv[:, pl.ds(pl.multiple_of(OWN + PIECE * zq, 32), PIECE), :] = kvsend[qz]
    for k in range(4):
        @pl.when(k == zq)
        def _():
            kv[:, 128 * k : 128 * k + 128, :] = skv_ref[...]

        @pl.when(k > zq)
        def _():
            kv[:, 128 * k : 128 * k + 128, :] = jnp.zeros((2, 128, HEAD), BF16)

    @pl.when(same)
    def _():
        wbuf[ctx] = w_ref[...]

    mst[...] = jnp.full(mst.shape, -1e30, F32)
    lst[...] = jnp.zeros(lst.shape, F32)
    acc[...] = jnp.zeros(acc.shape, F32)

    def link(idx, to):
        rows = kvrows(CHAIN + PIECE * idx)
        return rcopy(rows, rows, s_chain.at[idx // 6], r_chain.at[idx], dev(to, y, x, c))

    def chain(slot):
        for i, base, ok, to in (
            (slot - LAG * zq, 0, zq < 3, z + 1), (slot - LAG * (3 - zq), 6, zq > 0, z - 1)
        ):
            @pl.when(jnp.logical_and(i >= 0, i < 6))
            def _():
                cp = link(base + i, to)
                cp.wait_recv()
                pl.when(ok)(cp.start)

    def chain_sent():
        for n, ok in enumerate((zq < 3, zq > 0)):
            every = kvrows(CHAIN, 6 * PIECE)
            pl.when(ok)(rcopy(every, every, s_chain.at[n], r_chain.at[0], me).wait_send)

    sib = dev(z, y, x, 1 - c)

    def wpart(origin, j, cc):
        per = PARTS // 2
        rows = 64 // per
        first = pl.multiple_of(rows * (j % per), rows)
        return wbuf.at[4 * ((origin + 32) % 16) + 2 * cc + j // per, pl.ds(first, rows)]

    def wsend(e, way):
        t, j = e // PARTS, e % PARTS
        part = wpart(z - t if way else z + t, j, c)
        ssem, rsem = (s_w.at[0], r_wp) if way else (s_w.at[1], r_wm)
        return rcopy(part, part, ssem, rsem.at[e], dev((z + (1 if way else 15)) % 16, y, x, c))

    def wshare(t, way):
        block = wbuf.at[pl.ds(4 * (((z - t if way else z + t) + 32) % 16) + 2 * c, 2)]
        return rcopy(block, block, s_w.at[2], r_ws.at[0], sib)

    def wstart():
        def one(e, _):
            wsend(e, True).start()
            wsend(e, False).start()
            return 0

        lax.fori_loop(0, PARTS, one, 0)

    def wevents(first, last):
        def one(e, _):
            wsend(e, True).wait_recv()
            pl.when(e < 7 * PARTS)(wsend(e + PARTS, True).start)

            @pl.when(e < 7 * PARTS)
            def _():
                wsend(e, False).wait_recv()
                pl.when(e < 6 * PARTS)(wsend(e + PARTS, False).start)

            @pl.when(e % PARTS == PARTS - 1)
            def _():
                wshare(e // PARTS + 1, True).start()
                pl.when(e < 7 * PARTS)(wshare(e // PARTS + 1, False).start)

            return 0

        lax.fori_loop(first, last, one, 0)

    def wfinish():
        every = wbuf.at[pl.ds(0, 30)]
        rcopy(every, every, s_w.at[2], r_ws.at[0], sib).wait_recv()

    def wsent():
        for n, count in enumerate((16, 14, 30)):
            every = wbuf.at[pl.ds(0, count)]
            rcopy(every, every, s_w.at[n], r_ws.at[0], sib).wait_send()

    def attend(first, count, masked=False):
        rows = pl.ds(first if isinstance(first, int) else pl.multiple_of(first, 32), count)
        q = qbuf[...].reshape(HEADS * 512, HEAD)
        s = lax.dot_general(kv[0, rows], q, (((1,), (1,)), ((), ())), preferred_element_type=F32)
        if masked:
            key = lax.broadcasted_iota(jnp.int32, s.shape, 0)
            row = lax.broadcasted_iota(jnp.int32, s.shape, 1) % 512
            pos = (key // 128) * 512 + y * 128 + key % 128
            s = jnp.where(pos <= row + 512 * zq, s, -jnp.inf)
        before = mst[...]
        top = jnp.maximum(before, jnp.max(s, axis=0, keepdims=True))
        p = jnp.exp2((s - top) * SCALE_LOG2)
        shrink = jnp.exp2((before - top) * SCALE_LOG2)
        mst[...] = top
        lst[...] = lst[...] * shrink + jnp.sum(p, axis=0, keepdims=True)
        acc[...] = acc[...] * shrink + lax.dot_general(
            kv[1, rows], p.astype(BF16), (((0,), (0,)), ((), ())), preferred_element_type=F32
        )

    half = 3 * PIECE
    at = 0
    one_way = CHAIN + 6 * PIECE * (zq // 2)
    other_way = CHAIN + 6 * PIECE * (1 - zq // 2)
    def w0_wait(first):
        for k in range(2):
            yy = first + k
            cp = rcopy(w_ref, wbuf.at[4 * z + yy], s_w0.at[0], r_w0.at[yy], me)
            pl.when(jnp.logical_not(jnp.logical_and(same, yy == y)))(cp.wait_recv)

    def got_queries():
        for cp in qs:
            cp.wait_recv()

    def got_own():
        for cp in own:
            cp.wait_recv()

    def got_near():
        for d in (1, 2, 3):
            pl.when(zq >= d)(near[d - 1].wait_recv)

    def ring_begin():
        w0_wait(2 * c)
        wstart()

    work = {
        "w": w0_send, "q": got_queries, "o": got_own, "n": got_near, "r": ring_begin,
        "O": lambda: attend(OWN, 4 * PIECE),
        "N": lambda: attend(NEAR, 512, True),
        "A": lambda: attend(one_way, half),
        "B": lambda: attend(other_way, half),
        "C": lambda: attend(one_way + half, half),
        "D": lambda: attend(other_way + half, half),
    }
    for slot, (events, todo) in enumerate(SLOTS):
        if slot < 6 + 3 * LAG:
            chain(slot)
        for name in todo.split():
            work[name]()
        wevents(at, at + events)
        at += events

    ocp, scp = [], []
    for r in range(4):
        for h in range(HEADS):
            cols = slice(512 * h + 128 * r, 512 * h + 128 * r + 128)
            ost[r, h] = mst[:, cols]
            ost[r, HEADS + h] = lst[:, cols]
    for d in (2, 1, 3):
        r = (y + d) % 4
        scp.append(rcopy(ost.at[r], ostr.at[d - 1], s_st.at[d - 1], r_st.at[d - 1], dev(z, r, x, c)))
        scp[-1].start()
    for k in range(2):
        for h in (2 * k, 2 * k + 1):
            cols = slice(512 * h, 512 * h + 512)
            o = acc[:, cols] * (1.0 / lst[:, cols])
            for r in range(4):
                obuf[k, r, h % 2] = o[:, r * 128 : r * 128 + 128].astype(BF16)
        for d in (2, 1, 3):
            r, n = (y + d) % 4, 3 * k + d - 1
            ocp.append(rcopy(obuf.at[k, r], orecv.at[k, d - 1], s_o.at[n], r_o.at[n], dev(z, r, x, c)))
            ocp[-1].start()
        wevents(at, at + MID[k])
        at += MID[k]

    for k in range(2):
        for cp in (scp if k == 0 else []) + ocp[3 * k : 3 * k + 3]:
            cp.wait_recv()
        for h in range(2):
            ms = [ost[y, 2 * k + h]] + [ostr[n, 2 * k + h] for n in range(3)]
            ls = [ost[y, HEADS + 2 * k + h]] + [ostr[n, HEADS + 2 * k + h] for n in range(3)]
            os_ = [obuf[k, y, h]] + [orecv[k, n, h] for n in range(3)]
            top = jnp.maximum(jnp.maximum(ms[0], ms[1]), jnp.maximum(ms[2], ms[3]))
            ws = [l * jnp.exp2((m - top) * SCALE_LOG2) for m, l in zip(ms, ls)]
            inv = 1.0 / (ws[0] + ws[1] + ws[2] + ws[3])
            o = sum(o_.astype(F32) * (w * inv) for o_, w in zip(os_, ws))
            o = o.T.astype(BF16)
            abuf_out[k, :, h * HEAD : h * HEAD + HEAD] = o
            att_ref[:, (2 * k + h) * HEAD : (2 * k + h + 1) * HEAD] = o
        for d in (2, 1, 3, 0):
            for t in range(2):
                to = dev(z, ypair if t == 0 else y, (x + d) % 4, py)
                cp = rcopy(abuf_out.at[k], abuf.at[tp, k], s_a.at[0], r_a.at[0], to)
                if d == 0 and t == 1:
                    pl.when(jnp.logical_not(same))(cp.start)
                else:
                    cp.start()

        @pl.when(same)
        def _():
            abuf[tp, k] = abuf_out[k]

        wevents(at, at + LATE[k])
        at += LATE[k]

    wevents(at, 8 * PARTS)
    w0_wait(2 * (1 - c))
    wfinish()
    def every_a(count):
        return rcopy(abuf.at[pl.ds(0, count)], abuf.at[pl.ds(0, count)], s_a.at[0], r_a.at[0], sib)

    pl.when(same)(every_a(7).wait_recv)
    pl.when(jnp.logical_not(same))(every_a(8).wait_recv)

    def project(g, total):
        for k in range(2):
            w = wbuf[pl.ds(8 * g + 4 * k, 4)].reshape(256, 512)
            total = total + jnp.dot(abuf[g, k], w, preferred_element_type=F32)
        return total

    res[...] = lax.fori_loop(0, 8, project, jnp.zeros((128, 512), F32)).astype(BF16)
    out = rcopy(res, resrecv, s_out.at[0], r_out.at[0], dev(z, ypair, x, 1 - c))

    @pl.when(same)
    def _():
        mix_ref[...] = res[...]

    @pl.when(jnp.logical_not(same))
    def _():
        out.start()
        out.wait()
        mix_ref[...] = resrecv[...]

    for cp in far + qs + own + scp + ocp:
        cp.wait_send()
    for d in (1, 2, 3):
        pl.when(zq + d < 4)(near[d - 1].wait_send)
    for cp, ns in w0:
        pl.when(ns)(cp.wait_send)
    chain_sent()
    pl.when(same)(every_a(7).wait_send)
    pl.when(jnp.logical_not(same))(every_a(8).wait_send)
    wsent()


def hand_over(att_in, mix_in, att_out, mix_out):
    att_out[...] = att_in[...]
    mix_out[...] = mix_in[...]


def body(queries, stretch_key_value, cache_kv, chosen, out_weight):
    dma = lambda n: pltpu.SemaphoreType.DMA((n,))
    vmem = pl.BlockSpec(memory_space=pltpu.VMEM)
    results = pl.pallas_call(
        kernel,
        out_shape=(jax.ShapeDtypeStruct((128, 512), BF16), jax.ShapeDtypeStruct((128, 512), BF16)),
        in_specs=[vmem, vmem, vmem, pl.BlockSpec(memory_space=pltpu.SMEM), vmem],
        out_specs=(vmem, vmem),
        scratch_shapes=[
            pltpu.VMEM((4, 2, PIECE, HEAD), BF16),
            pltpu.VMEM((2, 2048, HEAD), BF16),
            pltpu.VMEM((HEADS, 128, HEAD), BF16),
            pltpu.VMEM((HEADS, 512, HEAD), BF16),
            pltpu.VMEM((HEAD, HEADS * 512), F32),
            pltpu.VMEM((1, HEADS * 512), F32),
            pltpu.VMEM((1, HEADS * 512), F32),
            pltpu.VMEM((2, 4, 2, HEAD, 128), BF16),
            pltpu.VMEM((4, 2 * HEADS, 1, 128), F32),
            pltpu.VMEM((2, 3, 2, HEAD, 128), BF16),
            pltpu.VMEM((3, 2 * HEADS, 1, 128), F32),
            pltpu.VMEM((8, 2, 128, 256), BF16),
            pltpu.VMEM((2, 128, 256), BF16),
            pltpu.VMEM((64, 64, 512), BF16),
            pltpu.VMEM((128, 512), BF16),
            pltpu.VMEM((128, 512), BF16),
        ]
        + [dma(n) for n in (3, 3, 3, 2, 3, 6, 3, 1, 4, 3, 1)]
        + [dma(n) for n in (3, 3, 12, 3, 6, 3, 1, 4, 8 * PARTS, 7 * PARTS, 1, 1)],
        compiler_params=pltpu.CompilerParams(
            collective_id=0, has_side_effects=True, vmem_limit_bytes=56 * 2**20
        ),
        cost_estimate=pl.CostEstimate(flops=2 * 2**30, bytes_accessed=4 * 2**20, transcendentals=2**22),
    )(queries, stretch_key_value, cache_kv, chosen.transpose(2, 0, 1), out_weight)
    return pl.pallas_call(
        hand_over,
        out_shape=tuple(jax.ShapeDtypeStruct(r.shape, r.dtype) for r in results),
        in_specs=[vmem, vmem],
        out_specs=(vmem, vmem),
    )(*results)


def solution(mesh):
    in_specs = (
        P("ctx", "tp"),
        P(None, "ctx", "tp"),
        P(None, None, "ctx", "tp"),
        P(),
        P("ctx", "tp"),
    )
    out_specs = (P("ctx", "tp"), P("ctx", "tp"))
    return jax.shard_map(body, mesh=mesh, in_specs=in_specs, out_specs=out_specs, check_vma=False)
```

```python
import math

import jax
import jax.numpy as jnp
from jax import lax
from jax.experimental import pallas as pl
from jax.experimental.pallas import tpu as pltpu
from jax.sharding import PartitionSpec as P

MESH = pl.DeviceIdType.MESH
HEAD = 128
HEADS = 4
SCALE_LOG2 = math.log2(math.e) / math.sqrt(HEAD)
PIECE = 96
NEAR, OWN, CHAIN = 0, 512, 896
PARTS = 2
SLOTS = ((0,"w"),(0,""),(0,""),(0,""),(0,"q o O"),(0,"r n"),(0,"N"),(1,""),(0,"A"),(1,""),(0,"C"),(1,""),(0,"B"),(1,""),(0,""),(1,"D"))
LAG = 3
MID, LATE = (1,3), (3,3)
BF16, F32 = jnp.bfloat16, jnp.float32


def kernel(
    q_ref, skv_ref, cache_hbm, chosen_ref, w_ref, att_ref, mix_ref,
    cache_ref, cache_sem, kvsend, kv, qsend, qbuf, acc, mst, lst, obuf, ost, orecv, ostr, abuf, abuf_out, wbuf, res, resrecv,
    s_far, s_own, s_near, s_chain, s_q, s_o, s_st, s_a, s_w0, s_w, s_out,
    r_own, r_near, r_chain, r_q, r_o, r_st, r_a, r_w0, r_wp, r_wm, r_ws, r_out,
):
    ctx, tp = lax.axis_index("ctx"), lax.axis_index("tp")
    z, y, x, c = ctx // 4, ctx % 4, tp // 2, tp % 2
    qz, zq = z // 4, z % 4
    py = y % 2
    ypair = y + 1 - 2 * py
    same = c == py

    def dev(zz, yy, xx, cc):
        return (zz * 4 + yy, xx * 2 + cc)

    def rcopy(src, dst, ssem, rsem, to):
        return pltpu.make_async_remote_copy(
            src_ref=src, dst_ref=dst, send_sem=ssem, recv_sem=rsem, device_id=to, device_id_type=MESH
        )

    me = dev(z, y, x, c)

    fetch = pltpu.make_async_copy(cache_hbm, cache_ref, cache_sem)
    fetch.start()

    barrier = pltpu.get_barrier_semaphore()

    def greet(to):
        pl.semaphore_signal(barrier, inc=1, device_id=to, device_id_type=MESH)

    for d in range(1, 4):
        greet(dev(4 * qz + (zq + d) % 4, y, x, c))
        greet(dev(z, (y + d) % 4, x, c))
    greet(dev((z + 1) % 16, y, x, c))
    greet(dev((z + 15) % 16, y, x, c))
    greet(dev(z, y, x, 1 - c))

    @pl.when(zq == 0)
    def _():
        for k in range(4):
            greet(dev(4 * ((qz + 3) % 4) + k, y, x, c))
        for k in (2, 3):
            greet(dev(4 * ((qz + 2) % 4) + k, y, x, c))

    @pl.when(zq == 3)
    def _():
        for k in range(4):
            greet(dev(4 * ((qz + 1) % 4) + k, y, x, c))
        for k in (0, 1):
            greet(dev(4 * ((qz + 2) % 4) + k, y, x, c))

    mine = y - py + c
    for d in range(4):
        yy = (y + d) % 4
        if d == 0:
            @pl.when(jnp.logical_not(same))
            def _():
                greet(dev(z, yy, x, py))
        else:
            greet(dev(z, yy, x, py))
        xx = (x + d) % 4
        for k in range(2):
            if d == 0:
                @pl.when(jnp.logical_not(jnp.logical_and(same, k == c)))
                def _():
                    greet(dev(z, mine, xx, k))
            else:
                greet(dev(z, mine, xx, k))
    mst[...] = jnp.full(mst.shape, -1e30, F32)
    lst[...] = jnp.zeros(lst.shape, F32)
    acc[...] = jnp.zeros(acc.shape, F32)
    for h in range(HEADS):
        qsend[h] = q_ref[:, h * HEAD : h * HEAD + HEAD]
    pl.semaphore_wait(barrier, 24 - 2 * same.astype(jnp.int32))

    fetch.wait()

    for b in range(4):
        for j in range(3):
            idx = chosen_ref[j, b, tp]
            kvsend[b, 0, 32 * j : 32 * j + 32] = cache_ref[0, idx]
            kvsend[b, 1, 32 * j : 32 * j + 32] = cache_ref[1, idx]

    def kvrows(first, count=PIECE):
        return kv.at[:, pl.ds(pl.multiple_of(first, 32), count), :]

    up = zq // 2
    far = [
        ((qz + 1) % 4, 0, 3 - zq),
        ((qz + 3) % 4, 3, 6 + zq),
        ((qz + 2) % 4, 3 * (1 - up), up * (7 - zq) + (1 - up) * (10 + zq)),
    ]
    far = [
        rcopy(kvsend.at[b], kvrows(CHAIN + PIECE * i), s_far.at[n], r_chain.at[i], dev(4 * b + e, y, x, c))
        for n, (b, e, i) in enumerate(far)
    ]
    for n in (2, 0, 1):
        far[n].start()
    my_rows = qbuf.at[:, pl.ds(pl.multiple_of(128 * y, 128), 128), :]
    qs = [
        rcopy(qsend, my_rows, s_q.at[d - 1], r_q.at[d - 1], dev(z, (y + d) % 4, x, c)) for d in (1, 2, 3)
    ]
    for cp in qs:
        cp.start()
    own = [
        rcopy(
            kvsend.at[qz], kvrows(OWN + PIECE * zq), s_own.at[d - 1], r_own.at[d - 1],
            dev(4 * qz + (zq + d) % 4, y, x, c),
        )
        for d in (1, 2, 3)
    ]
    for cp in own:
        cp.start()
    near = [
        rcopy(
            skv_ref, kvrows(NEAR + 128 * zq, 128), s_near.at[d - 1], r_near.at[d - 1],
            dev(4 * qz + (zq + d) % 4, y, x, c),
        )
        for d in (1, 2, 3)
    ]
    for d in (1, 2, 3):
        pl.when(zq + d < 4)(near[d - 1].start)
    w0 = []
    for t in range(2):
        for k in range(2):
            yy = c + 2 * t
            cp = rcopy(w_ref, wbuf.at[ctx], s_w0.at[2 * t + k], r_w0.at[y], dev(z, yy, x, k))
            w0.append((cp, jnp.logical_not(jnp.logical_and(yy == y, k == c))))

    def w0_send():
        for cp, notself in w0:
            pl.when(notself)(cp.start)

    qbuf[:, pl.ds(pl.multiple_of(128 * y, 128), 128), :] = qsend[...]
    kv[:, pl.ds(pl.multiple_of(OWN + PIECE * zq, 32), PIECE), :] = kvsend[qz]
    for k in range(4):
        @pl.when(k == zq)
        def _():
            kv[:, 128 * k : 128 * k + 128, :] = skv_ref[...]

        @pl.when(k > zq)
        def _():
            kv[:, 128 * k : 128 * k + 128, :] = jnp.zeros((2, 128, HEAD), BF16)

    @pl.when(same)
    def _():
        wbuf[ctx] = w_ref[...]


    def link(idx, to):
        rows = kvrows(CHAIN + PIECE * idx)
        return rcopy(rows, rows, s_chain.at[idx // 6], r_chain.at[idx], dev(to, y, x, c))

    def chain(slot):
        for i, base, ok, to in (
            (slot - LAG * zq, 0, zq < 3, z + 1), (slot - LAG * (3 - zq), 6, zq > 0, z - 1)
        ):
            @pl.when(jnp.logical_and(i >= 0, i < 6))
            def _():
                cp = link(base + i, to)
                cp.wait_recv()
                pl.when(ok)(cp.start)

    def chain_sent():
        for n, ok in enumerate((zq < 3, zq > 0)):
            every = kvrows(CHAIN, 6 * PIECE)
            pl.when(ok)(rcopy(every, every, s_chain.at[n], r_chain.at[0], me).wait_send)

    sib = dev(z, y, x, 1 - c)

    def wpart(origin, j, cc):
        per = PARTS // 2
        rows = 64 // per
        first = pl.multiple_of(rows * (j % per), rows)
        return wbuf.at[4 * ((origin + 32) % 16) + 2 * cc + j // per, pl.ds(first, rows)]

    def wsend(e, way):
        t, j = e // PARTS, e % PARTS
        part = wpart(z - t if way else z + t, j, c)
        ssem, rsem = (s_w.at[0], r_wp) if way else (s_w.at[1], r_wm)
        return rcopy(part, part, ssem, rsem.at[e], dev((z + (1 if way else 15)) % 16, y, x, c))

    def wshare(t, way):
        block = wbuf.at[pl.ds(4 * (((z - t if way else z + t) + 32) % 16) + 2 * c, 2)]
        return rcopy(block, block, s_w.at[2], r_ws.at[0], sib)

    def wstart():
        def one(e, _):
            wsend(e, True).start()
            wsend(e, False).start()
            return 0

        lax.fori_loop(0, PARTS, one, 0)

    def wevents(first, last):
        def one(e, _):
            wsend(e, True).wait_recv()
            pl.when(e < 7 * PARTS)(wsend(e + PARTS, True).start)

            @pl.when(e < 7 * PARTS)
            def _():
                wsend(e, False).wait_recv()
                pl.when(e < 6 * PARTS)(wsend(e + PARTS, False).start)

            @pl.when(e % PARTS == PARTS - 1)
            def _():
                wshare(e // PARTS + 1, True).start()
                pl.when(e < 7 * PARTS)(wshare(e // PARTS + 1, False).start)

            return 0

        lax.fori_loop(first, last, one, 0)

    def wfinish():
        every = wbuf.at[pl.ds(0, 30)]
        rcopy(every, every, s_w.at[2], r_ws.at[0], sib).wait_recv()

    def wsent():
        for n, count in enumerate((16, 14, 30)):
            every = wbuf.at[pl.ds(0, count)]
            rcopy(every, every, s_w.at[n], r_ws.at[0], sib).wait_send()

    def attend(first, count, masked=False):
        rows = pl.ds(first if isinstance(first, int) else pl.multiple_of(first, 32), count)
        q = qbuf[...].reshape(HEADS * 512, HEAD)
        s = lax.dot_general(kv[0, rows], q, (((1,), (1,)), ((), ())), preferred_element_type=F32)
        if masked:
            key = lax.broadcasted_iota(jnp.int32, s.shape, 0)
            row = lax.broadcasted_iota(jnp.int32, s.shape, 1) % 512
            pos = (key // 128) * 512 + y * 128 + key % 128
            s = jnp.where(pos <= row + 512 * zq, s, -jnp.inf)
        before = mst[...]
        top = jnp.maximum(before, jnp.max(s, axis=0, keepdims=True))
        p = jnp.exp2((s - top) * SCALE_LOG2)
        shrink = jnp.exp2((before - top) * SCALE_LOG2)
        mst[...] = top
        lst[...] = lst[...] * shrink + jnp.sum(p, axis=0, keepdims=True)
        acc[...] = acc[...] * shrink + lax.dot_general(
            kv[1, rows], p.astype(BF16), (((0,), (0,)), ((), ())), preferred_element_type=F32
        )

    half = 3 * PIECE
    at = 0
    one_way = CHAIN + 6 * PIECE * (zq // 2)
    other_way = CHAIN + 6 * PIECE * (1 - zq // 2)
    def w0_wait(first):
        for k in range(2):
            yy = first + k
            cp = rcopy(w_ref, wbuf.at[4 * z + yy], s_w0.at[0], r_w0.at[yy], me)
            pl.when(jnp.logical_not(jnp.logical_and(same, yy == y)))(cp.wait_recv)

    def got_queries():
        for cp in qs:
            cp.wait_recv()

    def got_own():
        for cp in own:
            cp.wait_recv()

    def got_near():
        for d in (1, 2, 3):
            pl.when(zq >= d)(near[d - 1].wait_recv)

    def ring_begin():
        w0_wait(2 * c)
        wstart()

    work = {
        "w": w0_send, "q": got_queries, "o": got_own, "n": got_near, "r": ring_begin,
        "O": lambda: attend(OWN, 4 * PIECE),
        "N": lambda: attend(NEAR, 512, True),
        "A": lambda: attend(one_way, half),
        "B": lambda: attend(other_way, half),
        "C": lambda: attend(one_way + half, half),
        "D": lambda: attend(other_way + half, half),
    }
    for slot, (events, todo) in enumerate(SLOTS):
        if slot < 6 + 3 * LAG:
            chain(slot)
        for name in todo.split():
            work[name]()
        wevents(at, at + events)
        at += events

    ocp, scp = [], []
    for r in range(4):
        for h in range(HEADS):
            cols = slice(512 * h + 128 * r, 512 * h + 128 * r + 128)
            ost[r, h] = mst[:, cols]
            ost[r, HEADS + h] = lst[:, cols]
    for d in (2, 1, 3):
        r = (y + d) % 4
        scp.append(rcopy(ost.at[r], ostr.at[d - 1], s_st.at[d - 1], r_st.at[d - 1], dev(z, r, x, c)))
        scp[-1].start()
    for k in range(2):
        for h in (2 * k, 2 * k + 1):
            cols = slice(512 * h, 512 * h + 512)
            o = acc[:, cols] * (1.0 / lst[:, cols])
            for r in range(4):
                obuf[k, r, h % 2] = o[:, r * 128 : r * 128 + 128].astype(BF16)
        for d in (2, 1, 3):
            r, n = (y + d) % 4, 3 * k + d - 1
            ocp.append(rcopy(obuf.at[k, r], orecv.at[k, d - 1], s_o.at[n], r_o.at[n], dev(z, r, x, c)))
            ocp[-1].start()
        wevents(at, at + MID[k])
        at += MID[k]

    for k in range(2):
        for cp in (scp if k == 0 else []) + ocp[3 * k : 3 * k + 3]:
            cp.wait_recv()
        for h in range(2):
            ms = [ost[y, 2 * k + h]] + [ostr[n, 2 * k + h] for n in range(3)]
            ls = [ost[y, HEADS + 2 * k + h]] + [ostr[n, HEADS + 2 * k + h] for n in range(3)]
            os_ = [obuf[k, y, h]] + [orecv[k, n, h] for n in range(3)]
            top = jnp.maximum(jnp.maximum(ms[0], ms[1]), jnp.maximum(ms[2], ms[3]))
            ws = [l * jnp.exp2((m - top) * SCALE_LOG2) for m, l in zip(ms, ls)]
            inv = 1.0 / (ws[0] + ws[1] + ws[2] + ws[3])
            o = sum(o_.astype(F32) * (w * inv) for o_, w in zip(os_, ws))
            o = o.T.astype(BF16)
            abuf_out[k, :, h * HEAD : h * HEAD + HEAD] = o
            att_ref[:, (2 * k + h) * HEAD : (2 * k + h + 1) * HEAD] = o
        for d in (2, 1, 3, 0):
            for t in range(2):
                to = dev(z, ypair if t == 0 else y, (x + d) % 4, py)
                cp = rcopy(abuf_out.at[k], abuf.at[tp, k], s_a.at[0], r_a.at[0], to)
                if d == 0 and t == 1:
                    pl.when(jnp.logical_not(same))(cp.start)
                else:
                    cp.start()

        @pl.when(same)
        def _():
            abuf[tp, k] = abuf_out[k]

        wevents(at, at + LATE[k])
        at += LATE[k]

    wevents(at, 8 * PARTS)
    w0_wait(2 * (1 - c))
    wfinish()
    def every_a(count):
        return rcopy(abuf.at[pl.ds(0, count)], abuf.at[pl.ds(0, count)], s_a.at[0], r_a.at[0], sib)

    pl.when(same)(every_a(7).wait_recv)
    pl.when(jnp.logical_not(same))(every_a(8).wait_recv)

    def project(g, total):
        for k in range(2):
            w = wbuf[pl.ds(8 * g + 4 * k, 4)].reshape(256, 512)
            total = total + jnp.dot(abuf[g, k], w, preferred_element_type=F32)
        return total

    res[...] = lax.fori_loop(0, 8, project, jnp.zeros((128, 512), F32)).astype(BF16)
    out = rcopy(res, resrecv, s_out.at[0], r_out.at[0], dev(z, ypair, x, 1 - c))

    @pl.when(same)
    def _():
        mix_ref[...] = res[...]

    @pl.when(jnp.logical_not(same))
    def _():
        out.start()
        out.wait()
        mix_ref[...] = resrecv[...]

    for cp in far + qs + own + scp + ocp:
        cp.wait_send()
    for d in (1, 2, 3):
        pl.when(zq + d < 4)(near[d - 1].wait_send)
    for cp, ns in w0:
        pl.when(ns)(cp.wait_send)
    chain_sent()
    pl.when(same)(every_a(7).wait_send)
    pl.when(jnp.logical_not(same))(every_a(8).wait_send)
    wsent()


def hand_over(att_in, mix_in, att_out, mix_out):
    att_out[...] = att_in[...]
    mix_out[...] = mix_in[...]


def body(queries, stretch_key_value, cache_kv, chosen, out_weight):
    dma = lambda n: pltpu.SemaphoreType.DMA((n,))
    vmem = pl.BlockSpec(memory_space=pltpu.VMEM)
    results = pl.pallas_call(
        kernel,
        out_shape=(jax.ShapeDtypeStruct((128, 512), BF16), jax.ShapeDtypeStruct((128, 512), BF16)),
        in_specs=[
            vmem, vmem, pl.BlockSpec(memory_space=pl.ANY), pl.BlockSpec(memory_space=pltpu.SMEM), vmem
        ],
        out_specs=(vmem, vmem),
        scratch_shapes=[
            pltpu.VMEM((2, 128, 32, HEAD), BF16),
            pltpu.SemaphoreType.DMA,
            pltpu.VMEM((4, 2, PIECE, HEAD), BF16),
            pltpu.VMEM((2, 2048, HEAD), BF16),
            pltpu.VMEM((HEADS, 128, HEAD), BF16),
            pltpu.VMEM((HEADS, 512, HEAD), BF16),
            pltpu.VMEM((HEAD, HEADS * 512), F32),
            pltpu.VMEM((1, HEADS * 512), F32),
            pltpu.VMEM((1, HEADS * 512), F32),
            pltpu.VMEM((2, 4, 2, HEAD, 128), BF16),
            pltpu.VMEM((4, 2 * HEADS, 1, 128), F32),
            pltpu.VMEM((2, 3, 2, HEAD, 128), BF16),
            pltpu.VMEM((3, 2 * HEADS, 1, 128), F32),
            pltpu.VMEM((8, 2, 128, 256), BF16),
            pltpu.VMEM((2, 128, 256), BF16),
            pltpu.VMEM((64, 64, 512), BF16),
            pltpu.VMEM((128, 512), BF16),
            pltpu.VMEM((128, 512), BF16),
        ]
        + [dma(n) for n in (3, 3, 3, 2, 3, 6, 3, 1, 4, 3, 1)]
        + [dma(n) for n in (3, 3, 12, 3, 6, 3, 1, 4, 8 * PARTS, 7 * PARTS, 1, 1)],
        compiler_params=pltpu.CompilerParams(
            collective_id=0, has_side_effects=True, vmem_limit_bytes=56 * 2**20
        ),
        cost_estimate=pl.CostEstimate(flops=2 * 2**30, bytes_accessed=4 * 2**20, transcendentals=2**22),
    )(queries, stretch_key_value, cache_kv, chosen.transpose(2, 0, 1), out_weight)
    return pl.pallas_call(
        hand_over,
        out_shape=tuple(jax.ShapeDtypeStruct(r.shape, r.dtype) for r in results),
        in_specs=[vmem, vmem],
        out_specs=(vmem, vmem),
    )(*results)


def solution(mesh):
    in_specs = (
        P("ctx", "tp"),
        P(None, "ctx", "tp"),
        P(None, None, "ctx", "tp"),
        P(),
        P("ctx", "tp"),
    )
    out_specs = (P("ctx", "tp"), P("ctx", "tp"))
    return jax.shard_map(body, mesh=mesh, in_specs=in_specs, out_specs=out_specs, check_vma=False)
```
